512 devices in a mesh: ang: 4 (over y), gy: 32 (over z_lo, x, core), gx: 4 (over z_hi).
Axes of the slice: x: 4, y: 4, z: 16 (z_hi: 4, z_lo: 4; z = z_hi * 4 + z_lo), core: 2. Of those that a mesh axis runs over, the one named last changes fastest.
Arguments:
- spectrum_data: bfloat16 [2, 16, 256, 2048], P(None, None, 'gy', 'ang'), may hold values from -6 to 6
- offsets: int32 [2048], P('ang'), may hold values from 0 to 1020
- view_index: int32 [2048], P('ang'), may hold values from 0 to 1499
- kernel: float32 [4, 2048], P(None, 'ang'), may hold values from 0.25 to 1
- view_weight: float32 [1500], replicated, may hold values from 0.5 to 2
- volume: float32 [16, 256, 4096], P('ang', 'gy', 'gx'), may hold values from -6 to 6
- multiplier: float32 [16, 256, 4096], P('ang', 'gy', 'gx'), may hold values from -4 to 4
Outputs:
- denoised: float32 [16, 256, 4096], P('ang', 'gy', 'gx')
The draws below stay inside these ranges and needn't reach their ends.
Inputs may be any that keep to these rules, and one draw needn't show every extreme that they name: `offsets`: each offset is a cell of its sample's block of 1024 frequencies with the three cells after it in the block too.
All inputs are finite; a program needn't handle non-finite values.
Results may differ from the reference program's by a relative error of at most 0.0032.
Values sent between devices are 32-bit elements; how exact they have to be, the bound alone decides.
A program may use at most 64 MiB of HBM per device.

```python
import math
import jax
import jax.numpy as jnp
from jax import lax

NX = 4096
VIEWS = 1500
TAPS = 4
PLANES = 16
TV_STEPS = 4
SAMP_DEV = 512
NY = 256
KB = 1024
SAMPLES = 2048
N_ANG = 4


def with_ends(values, stream_key, smallest, high):
    dims = values.shape
    index_at = [jax.random.randint(jax.random.fold_in(stream_key, axis), (), 0, dims[axis]) for axis in range(len(dims))]
    values = values.at[tuple(index_at)].set(smallest)
    longest = dims.index(max(dims))
    index_at[longest] = (index_at[longest] + 1) % dims[longest]
    return values.at[tuple(index_at)].set(high)


def levels(key, shape, shards, least, largest):
    loudness, own = 1.0, jax.random.fold_in(key, 6)
    for position, parts in shards:
        steps = jnp.exp(jax.random.uniform(jax.random.fold_in(own, position), (parts,), jnp.float32, least / len(shards), largest / len(shards)))
        loudness = loudness * jnp.repeat(steps, shape[position] // parts).reshape([-1 if axis == position else 1 for axis in range(len(shape))])
    return loudness


def bell_draw(own_key, extent, scale, reach, cuts=(), kind=jnp.bfloat16):
    values = jax.random.normal(own_key, extent, jnp.float32) * scale
    if len(cuts) > 0:
        values = levels(own_key, extent, cuts, -0.22, 0.18) * values
    return jnp.clip(values, min=-reach, max=reach).astype(kind)


def setup_inputs(seed: int = 0) -> dict:
    seeds = jax.random.split(jax.random.key(seed), 8)
    spectrum_data = bell_draw(seeds[0], (2, PLANES, NY, SAMPLES), 1.0, 6.0, ((2, 32), (3, 4)))
    offsets = with_ends(jax.random.randint(seeds[1], (SAMPLES,), 0, KB - 3), jax.random.fold_in(seeds[1], 1), 0, (KB - 3) - 1).astype(jnp.int32)
    view_index = with_ends(jax.random.randint(seeds[2], (SAMPLES,), 0, VIEWS), jax.random.fold_in(seeds[2], 1), 0, VIEWS - 1).astype(jnp.int32)
    kernel = jnp.clip(0.25 + 0.75 * jax.random.uniform(seeds[3], (TAPS, SAMPLES), jnp.float32) ** levels(seeds[3], (TAPS, SAMPLES), ((1, 4),), -0.2, 0.2), 0.25, 1.0)
    view_weight = jnp.clip(jnp.exp(jax.random.uniform(seeds[4], (VIEWS,), jnp.float32, math.log(0.5), math.log(2.0))), 0.5, 2.0)
    volume = bell_draw(seeds[5], (PLANES, NY, NX), 1.0, 6.0, ((0, 4), (1, 32), (2, 4)), jnp.float32)
    multiplier = bell_draw(seeds[6], (PLANES, NY, NX), 0.5, 4.0, ((0, 4), (1, 32), (2, 4)), jnp.float32)
    return {"spectrum_data": spectrum_data, "offsets": offsets, "view_index": view_index, "kernel": kernel, "view_weight": view_weight, "volume": volume, "multiplier": multiplier}


smooth_weight = 0.5
dual_step = 1.0 / 12.0

def wave_table(freq_first, freq_count, cell_first, cell_count):
    freq_ids = freq_first + jnp.arange(freq_count, dtype=jnp.int32)
    cell_ids = cell_first + jnp.arange(cell_count, dtype=jnp.int32)
    phase_cells = freq_ids[:, None] * cell_ids[None, :] % NX
    phase_angle = phase_cells.astype(jnp.float32) * (2.0 * math.pi / NX)
    return jnp.concatenate([jnp.cos(phase_angle), -jnp.sin(phase_angle)], axis=0).astype(jnp.bfloat16)

def spread_blocks(offsets, view_index, kernel, view_weight):
    block_size = NX // N_ANG
    cell_ids = jnp.arange(block_size, dtype=jnp.int32)
    local_first = offsets.reshape(N_ANG, SAMP_DEV).astype(jnp.int32)
    kernel_rows = kernel.reshape(kernel.shape[0], N_ANG, SAMP_DEV)
    spread_sum = jnp.zeros((N_ANG, SAMP_DEV, block_size), jnp.float32)
    for tap_index in range(kernel.shape[0]):
        spread_sum = spread_sum + jnp.where(cell_ids[None, None, :] == (local_first + tap_index)[:, :, None], kernel_rows[tap_index][:, :, None], jnp.float32(0.0))
    weights = view_weight[view_index].reshape(N_ANG, SAMP_DEV)
    return (weights[:, :, None] * spread_sum).astype(jnp.bfloat16)

def divergence(flow_field):
    plane_part = flow_field[0] - jnp.pad(flow_field[0], ((1, 0), (0, 0), (0, 0)))[:-1]
    row_part = flow_field[1] - jnp.pad(flow_field[1], ((0, 0), (1, 0), (0, 0)))[:, :-1]
    cell_part = flow_field[2] - jnp.pad(flow_field[2], ((0, 0), (0, 0), (1, 0)))[:, :, :-1]
    return plane_part + row_part + cell_part

def slopes(values):
    slope_plane = jnp.pad(values[1:] - values[:-1], ((0, 1), (0, 0), (0, 0)))
    slope_row = jnp.pad(values[:, 1:] - values[:, :-1], ((0, 0), (0, 1), (0, 0)))
    slope_cell = jnp.pad(values[:, :, 1:] - values[:, :, :-1], ((0, 0), (0, 0), (0, 1)))
    return (slope_plane, slope_row, slope_cell)

def reference(spectrum_data, offsets, view_index, kernel, view_weight, volume, multiplier):
    spread = spread_blocks(offsets, view_index, kernel, view_weight).astype(jnp.float32)
    wave_rows = wave_table(0, NX, 0, NX).astype(jnp.float32)
    line_count = spectrum_data.shape[2]

    def one_plane(plane_data):
        grouped = plane_data.astype(jnp.float32).reshape(2 * line_count, N_ANG, SAMP_DEV)
        gridded = jnp.einsum('rbs,bsk->rbk', grouped, spread, precision=lax.Precision.HIGHEST)
        gridded = gridded.astype(jnp.bfloat16).reshape(2 * line_count, NX)
        joined = jnp.concatenate([gridded[:line_count], gridded[line_count:]], axis=1).astype(jnp.float32)
        return jnp.dot(joined, wave_rows, precision=lax.Precision.HIGHEST)
    back = lax.map(one_plane, jnp.moveaxis(spectrum_data, 1, 0)) * NX ** (-0.5)
    source = volume - back + multiplier
    scaled = source / smooth_weight
    flow_field = jnp.zeros((3,) + source.shape, jnp.float32)
    for repeat in range(TV_STEPS):
        slope_plane, slope_row, slope_cell = slopes(divergence(flow_field) - scaled)
        slope_norm = jnp.sqrt(slope_plane * slope_plane + slope_row * slope_row + slope_cell * slope_cell)
        flow_field = (flow_field + dual_step * jnp.stack([slope_plane, slope_row, slope_cell])) / (1.0 + dual_step * slope_norm)
    return source - smooth_weight * divergence(flow_field)
```

```python
import functools
import math

import jax
import jax.numpy as jnp
import numpy as np
from jax import lax
from jax.experimental import pallas as pl
from jax.experimental.pallas import tpu as pltpu
from jax.sharding import PartitionSpec as P

MESH = pl.DeviceIdType.MESH
TV_STEPS = 4
dual_step = 1.0 / 12.0
N_ANG = 4
HALO = 4


def wave_constants(length, columns):
    block = length // N_ANG
    width = columns // N_ANG
    freq = np.arange(length, dtype=np.int64)

    def rows(cells):
        phase = np.mod(freq[:, None] * cells[None, :], length)
        angle = phase.astype(np.float32) * np.float32(2.0 * math.pi / length)
        cos = np.cos(angle).reshape(N_ANG, block, -1)
        sin = np.sin(angle).reshape(N_ANG, block, -1)
        return np.concatenate([cos, -sin], axis=1).astype(jnp.bfloat16)

    main = rows(np.arange(columns)).reshape(N_ANG, 2 * block, N_ANG, width)
    edge_cells = np.zeros(128, np.int64)
    for b in range(N_ANG):
        edge_cells[8 * b : 8 * b + 4] = width * (b + 1) + np.arange(4)
        edge_cells[8 * b + 4 : 8 * b + 8] = width * b - 4 + np.arange(4)
    return np.ascontiguousarray(main.transpose(0, 2, 1, 3)), rows(edge_cells)


def body(
    sizes,
    data_hbm,
    offsets_hbm,
    views_hbm,
    taps_hbm,
    weights_hbm,
    volume_hbm,
    multiplier_hbm,
    wave_hbm,
    edge_hbm,
    out_ref,
    data,
    offsets,
    views,
    taps,
    weights,
    volume,
    multiplier,
    wave,
    edge,
    table,
    joined,
    vm_send,
    vm_tiles,
    vm_recv,
    vm_edge,
    part_send,
    part_recv,
    strip_send,
    strip_recv,
    turned,
    scaled,
    flows,
    masks,
    result,
    in_sem,
    vm_ssem,
    vm_rsem,
    ve_ssem,
    ve_rsem,
    pt_ssem,
    pt_rsem,
    st_ssem,
    st_rsem,
    hl_ssem,
    hl_rsem,
    out_ssem,
    out_rsem,
    own_sem,
):
    length, n_gy, n_gx = sizes
    block = length // N_ANG
    a, y, g = lax.axis_index("ang"), lax.axis_index("gy"), lax.axis_index("gx")
    peers = {d: lax.rem(a + d, N_ANG) for d in range(N_ANG)}

    barrier = pltpu.get_barrier_semaphore()

    def greet(where):
        pl.semaphore_signal(barrier, inc=1, device_id=where, device_id_type=MESH)

    for d in range(1, N_ANG):
        greet((peers[d], y, g))

    @pl.when(y > 0)
    def _():
        greet((a, y - 1, g))

    @pl.when(y < n_gy - 1)
    def _():
        greet((a, y + 1, g))

    @pl.when(jnp.logical_and(a == 0, g > 0))
    def _():
        for other in range(N_ANG):
            greet((other, y, g - 1))

    @pl.when(jnp.logical_and(a == N_ANG - 1, g < n_gx - 1))
    def _():
        for other in range(N_ANG):
            greet((other, y, g + 1))

    def fetch(src, dst, k):
        return pltpu.make_async_copy(src, dst, in_sem.at[k])

    small = [
        fetch(offsets_hbm, offsets, 0),
        fetch(views_hbm, views, 1),
        fetch(taps_hbm, taps, 2),
        fetch(weights_hbm, weights, 3),
        fetch(data_hbm, data, 4),
    ]
    fields = [fetch(volume_hbm, volume, 5), fetch(multiplier_hbm, multiplier, 6)]
    waves = {
        d: fetch(wave_hbm.at[a, peers[d]], wave.at[d], 7 + d) for d in range(N_ANG)
    }
    edges = fetch(edge_hbm.at[a], edge, 11)
    for copy in small + fields + [waves[2], waves[1], waves[3], edges, waves[0]]:
        copy.start()

    @pl.when(y == 0)
    def _():
        scaled[0:HALO] = jnp.zeros((HALO, 16, 384), jnp.float32)

    @pl.when(y == n_gy - 1)
    def _():
        scaled[8 + HALO :] = jnp.zeros((HALO, 16, 384), jnp.float32)

    lane = lax.broadcasted_iota(jnp.int32, (16, 384), 1)
    plane = lax.broadcasted_iota(jnp.int32, (16, 384), 0)
    first = jnp.logical_and(a == 0, g == 0)
    last = jnp.logical_and(a == N_ANG - 1, g == n_gx - 1)
    closed = jnp.logical_or(
        jnp.logical_and(lane == 383, first), jnp.logical_and(lane == 255, last)
    )
    masks[0] = jnp.where(closed, 0.0, dual_step)
    masks[1] = jnp.where(plane == 15, 0.0, dual_step)
    turned[...] = jnp.zeros((128, 128), jnp.float32)

    for copy in small:
        copy.wait()
    for h in range(11):
        table[h : h + 1, :] = weights[:, 128 * h : 128 * h + 128]
    tail = weights.shape[1] - 128
    table[11:12, :] = weights[:, tail : tail + 128]
    table[12:16, :] = jnp.zeros((4, 128), jnp.float32)
    full = table[...]
    high = full.astype(jnp.bfloat16)
    rest = full - high.astype(jnp.float32)
    mid = rest.astype(jnp.bfloat16)
    low = (rest - mid.astype(jnp.float32)).astype(jnp.bfloat16)
    ids = views[...]
    group = jnp.minimum(lax.shift_right_logical(ids, 7), 11)
    within = jnp.where(group == 11, ids - tail, ids - group * 128)
    hot = (lax.broadcasted_iota(jnp.int32, (128, 512), 0) == within).astype(jnp.float32)
    hot = hot.astype(jnp.bfloat16)
    picked = (
        jnp.dot(high, hot, preferred_element_type=jnp.float32)
        + jnp.dot(mid, hot, preferred_element_type=jnp.float32)
        + jnp.dot(low, hot, preferred_element_type=jnp.float32)
    )
    of_group = lax.broadcasted_iota(jnp.int32, (16, 512), 0) == group
    weight = jnp.sum(jnp.where(of_group, picked, 0.0), axis=0, keepdims=True)
    coefs = weight * taps[...]

    line_out = lax.broadcasted_iota(jnp.int32, (128, 128), 0)
    line_in = lax.broadcasted_iota(jnp.int32, (128, 128), 1)
    order = lax.rem(line_out, 16) * 8 + lax.div(line_out, 16)
    order = (line_in == order).astype(jnp.float32).astype(jnp.bfloat16)
    for c in range(2):
        data[128 * c : 128 * c + 128] = jnp.dot(
            order, data[128 * c : 128 * c + 128], preferred_element_type=jnp.float32
        ).astype(jnp.bfloat16)

    turn = g * (4 * 1024 // length)

    def grid_block(i, carry):
        base = pl.multiple_of(i * 256, 256)
        cell = lax.broadcasted_iota(jnp.int32, (256, 512), 0) + base
        away = cell - offsets[...]
        spread = jnp.zeros((256, 512), jnp.float32)
        for t in range(4):
            spread = jnp.where(away == t, coefs[t : t + 1], spread)
        gridded = lax.dot_general(
            data[...],
            spread.astype(jnp.bfloat16),
            (((1,), (1,)), ((), ())),
            preferred_element_type=jnp.float32,
        )
        re, im = gridded[:128], gridded[128:]
        quarter = jnp.bitwise_and(
            (lax.broadcasted_iota(jnp.int32, (1, 256), 1) + base) * turn, 3
        )
        odd = jnp.bitwise_and(quarter, 1) == 1
        re_sign = jnp.where(jnp.logical_or(quarter == 1, quarter == 2), -1.0, 1.0)
        im_sign = jnp.where(quarter >= 2, -1.0, 1.0)
        joined[:, pl.ds(base, 256)] = (jnp.where(odd, im, re) * re_sign).astype(jnp.bfloat16)
        joined[:, pl.ds(pl.multiple_of(base + block, 256), 256)] = (
            jnp.where(odd, re, im) * im_sign
        ).astype(jnp.bfloat16)
        return carry

    lax.fori_loop(0, block // 256, grid_block, 0)

    for copy in fields:
        copy.wait()
    low_lane = lax.broadcasted_iota(jnp.int32, (4, 8, 128), 2) < 64
    vm_send[...] = volume[...] + multiplier[...]
    for b in range(N_ANG):
        after = vm_send[:, :, pl.ds(256 * min(b + 1, 3), 128)]
        before = vm_send[:, :, pl.ds(256 * max(b, 1) - 128, 128)]
        vm_tiles[b] = jnp.where(low_lane, after, before)

    waves[2].wait()

    def transform(d):
        part_send[d] = jnp.dot(joined[...], wave[d], preferred_element_type=jnp.float32)

    transform(2)

    greeted = (
        N_ANG - 1
        + (y > 0).astype(jnp.int32)
        + (y < n_gy - 1).astype(jnp.int32)
        + (g > 0).astype(jnp.int32)
        + (g < n_gx - 1).astype(jnp.int32)
    )
    pl.semaphore_wait(barrier, greeted)

    def remote(src, dst, ssem, rsem, where):
        return pltpu.make_async_remote_copy(
            src_ref=src,
            dst_ref=dst,
            send_sem=ssem,
            recv_sem=rsem,
            device_id=where,
            device_id_type=MESH,
        )

    def part_copy(d, h):
        lines = pl.ds(64 * h, 64)
        return remote(
            part_send.at[d, lines],
            part_recv.at[d, lines],
            pt_ssem.at[d, h],
            pt_rsem.at[d, h],
            (peers[d], y, g),
        )

    def strip_copy(d):
        return remote(
            strip_send.at[peers[d]],
            strip_recv.at[d],
            st_ssem.at[d],
            st_rsem.at[d],
            (peers[d], y, g),
        )

    def vm_copies(d):
        mine = pl.ds(4 * a, 4)
        return [
            remote(
                vm_send.at[:, :, pl.ds(pl.multiple_of(256 * peers[d], 256), 256)],
                vm_recv.at[mine, :, pl.ds(0, 256)],
                vm_ssem.at[d, 0],
                vm_rsem.at[d, 0],
                (peers[d], y, g),
            ),
            remote(
                vm_tiles.at[peers[d]],
                vm_recv.at[mine, :, pl.ds(256, 128)],
                vm_ssem.at[d, 1],
                vm_rsem.at[d, 1],
                (peers[d], y, g),
            ),
        ]

    def vm_arrivals(d):
        theirs = pl.ds(4 * lax.rem(a + N_ANG - d, N_ANG), 4)
        return [
            remote(
                vm_send.at[:, :, pl.ds(0, 256)],
                vm_recv.at[theirs, :, pl.ds(0, 256)],
                vm_ssem.at[d, 0],
                vm_rsem.at[d, 0],
                (peers[d], y, g),
            ),
            remote(
                vm_tiles.at[0],
                vm_recv.at[theirs, :, pl.ds(256, 128)],
                vm_ssem.at[d, 1],
                vm_rsem.at[d, 1],
                (peers[d], y, g),
            ),
        ]

    def edge_copy(up, place, target):
        tile = 1024 - 128 if up else 0
        return remote(
            vm_send.at[:, :, pl.ds(tile, 128)],
            vm_edge.at[pl.ds(4 * place, 4)],
            ve_ssem.at[0 if up else 1],
            ve_rsem.at[place],
            target,
        )

    part_copy(2, 0).start()
    part_copy(2, 1).start()

    @pl.when(g < n_gx - 1)
    def _():
        edge_copy(True, a, (0, y, g + 1)).start()

    @pl.when(g > 0)
    def _():
        edge_copy(False, a, (N_ANG - 1, y, g - 1)).start()

    for d in (1, 3):
        waves[d].wait()
        transform(d)
        part_copy(d, 0).start()
        part_copy(d, 1).start()
    for d in (2, 1, 3):
        for copy in vm_copies(d):
            copy.start()
    edges.wait()
    strips = jnp.dot(joined[...], edge[...], preferred_element_type=jnp.float32)
    strips = jnp.transpose(strips)
    for b in range(N_ANG):
        strip_send[b] = strips[8 * b : 8 * b + 8]
    for d in (2, 1, 3):
        strip_copy(d).start()
    mine = pl.ds(4 * a, 4)
    vm_recv[mine, :, pl.ds(0, 256)] = vm_send[:, :, pl.ds(pl.multiple_of(256 * a, 256), 256)]
    vm_recv[mine, :, pl.ds(256, 128)] = vm_tiles[a]
    waves[0].wait()
    transform(0)

    for d in range(1, N_ANG):
        for copy in vm_arrivals(d):
            copy.wait_recv()
    takes_low = jnp.logical_and(a == 0, g > 0)
    takes_high = jnp.logical_and(a == N_ANG - 1, g < n_gx - 1)

    @pl.when(jnp.logical_or(takes_low, takes_high))
    def _():
        for place in range(N_ANG):
            edge_copy(True, place, (0, y, g)).wait_recv()
        at_low = lax.broadcasted_iota(jnp.int32, (16, 8, 128), 2) < 64
        swap = jnp.logical_xor(at_low, takes_low)
        vm_recv[:, :, pl.ds(256, 128)] = jnp.where(
            swap, vm_edge[...], vm_recv[:, :, pl.ds(256, 128)]
        )

    for half in range(2):
        for j in range(3):
            scaled[HALO : HALO + 8, pl.ds(8 * half, 8), pl.ds(128 * j, 128)] = jnp.swapaxes(
                vm_recv[pl.ds(8 * half, 8), :, pl.ds(128 * j, 128)], 0, 1
            )

    for d in range(1, N_ANG):
        strip_copy(d).wait_recv()
    strip = (strip_send[a] + strip_recv[1]) + (strip_recv[3] + strip_recv[2])
    sub = lax.broadcasted_iota(jnp.int32, (8, 128), 0)
    turned[0:8] = jnp.where(sub < 4, strip, 0.0)
    turned[120:128] = jnp.where(sub < 4, 0.0, strip)
    turned[...] = jnp.transpose(turned[...])
    unit = 2.0 * length**-0.5
    lower_dev, upper_dev = (a, y - 1, g), (a, y + 1, g)
    below = remote(
        scaled.at[pl.ds(HALO, HALO)],
        scaled.at[pl.ds(HALO + 8, HALO)],
        hl_ssem.at[0],
        hl_rsem.at[0],
        lower_dev,
    )
    above = remote(
        scaled.at[pl.ds(8, HALO)],
        scaled.at[pl.ds(0, HALO)],
        hl_ssem.at[1],
        hl_rsem.at[1],
        upper_dev,
    )
    for h in range(2):
        for d in range(1, N_ANG):
            part_copy(d, h).wait_recv()

        def settle(i, carry):
            lines = pl.ds(pl.multiple_of(16 * i, 16), 16)
            total = (part_send[0, lines] + part_recv[1, lines]) + (
                part_recv[3, lines] + part_recv[2, lines]
            )
            both = jnp.concatenate([total, turned[lines]], axis=1)
            own = scaled[HALO + i]
            scaled[HALO + i] = (own + own) - unit * both
            return carry

        lax.fori_loop(4 * h, 4 * h + 4, settle, 0)
        if h == 0:

            @pl.when(y > 0)
            def _():
                below.start()

        else:

            @pl.when(y < n_gy - 1)
            def _():
                above.start()

    top_row = 8 * y - HALO
    end_row = 8 * n_gy - 1

    def divergence(k, r):
        q0, q1, q2 = (flows[k, c, r] for c in range(3))
        below_plane = jnp.where(plane == 0, 0.0, pltpu.roll(q0, 1, 0))
        return (
            (q0 - below_plane) + (q1 - flows[k, 1, r - 1]) + (q2 - pltpu.roll(q2, 1, 1))
        )

    def target(k, r):
        if k == 0:
            return -scaled[r]
        return divergence(k - 1, r) - scaled[r]

    def sweep(k, start, count):
        def row(i, here):
            r = start + i
            up = target(k, r + 1)
            row_id = top_row + r
            closed_row = jnp.logical_or(row_id == -1, row_id == end_row)
            step_row = jnp.where(closed_row, 0.0, dual_step)
            g0 = (pltpu.roll(here, 15, 0) - here) * masks[1]
            g1 = (up - here) * step_row
            g2 = (pltpu.roll(here, 383, 1) - here) * masks[0]
            norm = jnp.sqrt((g0 * g0 + g1 * g1) + g2 * g2)
            scale = 1.0 / (1.0 + norm)
            for c, slope in enumerate((g0, g1, g2)):
                if k > 0:
                    slope = flows[k - 1, c, r] + slope
                flows[k, c, r] = slope * scale
            return up

        lax.fori_loop(0, count, row, target(k, start))

    for k in range(TV_STEPS):
        sweep(k, 4 + k, 7 - 2 * k)

    @pl.when(y > 0)
    def _():
        above.wait_recv()

    for k in range(TV_STEPS):
        sweep(k, k, 4)

    @pl.when(y < n_gy - 1)
    def _():
        below.wait_recv()

    for k in range(TV_STEPS):
        sweep(k, 11 - k, 4)

    def finish(i, carry):
        r = HALO + i
        scaled[r] = 0.5 * (scaled[r] - divergence(TV_STEPS - 1, r))
        return carry

    @pl.when(y > 0)
    def _():
        below.wait_send()

    @pl.when(y < n_gy - 1)
    def _():
        above.wait_send()

    lax.fori_loop(0, 8, finish, 0)
    for half in range(2):
        for j in range(2):
            result[pl.ds(8 * half, 8), :, pl.ds(128 * j, 128)] = jnp.swapaxes(
                scaled[HALO : HALO + 8, pl.ds(8 * half, 8), pl.ds(128 * j, 128)], 0, 1
            )

    def out_copy(d, column):
        return remote(
            result.at[pl.ds(4 * peers[d], 4)],
            out_ref.at[:, :, pl.ds(pl.multiple_of(256 * column, 256), 256)],
            out_ssem.at[d],
            out_rsem.at[d],
            (peers[d], y, g),
        )

    for d in (2, 1, 3):
        out_copy(d, a).start()
    own = pltpu.make_async_copy(
        result.at[pl.ds(4 * a, 4)],
        out_ref.at[:, :, pl.ds(pl.multiple_of(256 * a, 256), 256)],
        own_sem,
    )
    own.start()
    for d in range(1, N_ANG):
        part_copy(d, 0).wait_send()
        part_copy(d, 1).wait_send()
        strip_copy(d).wait_send()
        for copy in vm_copies(d):
            copy.wait_send()

    @pl.when(g < n_gx - 1)
    def _():
        edge_copy(True, a, (0, y, g)).wait_send()

    @pl.when(g > 0)
    def _():
        edge_copy(False, a, (0, y, g)).wait_send()

    own.wait()
    for d in range(1, N_ANG):
        out_copy(d, a).wait_send()
        out_copy(d, lax.rem(a + N_ANG - d, N_ANG)).wait_recv()


def per_device(sizes, spectrum_data, offsets, view_index, kernel, view_weight, volume, multiplier):
    length = sizes[0]
    columns = volume.shape[2]
    samples = offsets.shape[0]
    lines = 16 * 8
    main, edge = wave_constants(length, columns)
    block = length // N_ANG
    f32, bf16, i32 = jnp.float32, jnp.bfloat16, jnp.int32
    dma = pltpu.SemaphoreType.DMA
    views = view_weight.shape[0]
    scratch = [
        pltpu.VMEM((2 * lines, samples), bf16),
        pltpu.VMEM((1, samples), i32),
        pltpu.VMEM((1, samples), i32),
        pltpu.VMEM((4, samples), f32),
        pltpu.VMEM((1, views), f32),
        pltpu.VMEM((4, 8, columns), f32),
        pltpu.VMEM((4, 8, columns), f32),
        pltpu.VMEM((N_ANG, 2 * block, 256), bf16),
        pltpu.VMEM((2 * block, 128), bf16),
        pltpu.VMEM((16, 128), f32),
        pltpu.VMEM((lines, 2 * block), bf16),
        pltpu.VMEM((4, 8, columns), f32),
        pltpu.VMEM((N_ANG, 4, 8, 128), f32),
        pltpu.VMEM((16, 8, 384), f32),
        pltpu.VMEM((16, 8, 128), f32),
        pltpu.VMEM((N_ANG, lines, 256), f32),
        pltpu.VMEM((N_ANG, lines, 256), f32),
        pltpu.VMEM((N_ANG, 8, 128), f32),
        pltpu.VMEM((N_ANG, 8, 128), f32),
        pltpu.VMEM((128, 128), f32),
        pltpu.VMEM((16, 16, 384), f32),
        pltpu.VMEM((TV_STEPS, 3, 16, 16, 384), f32),
        pltpu.VMEM((2, 16, 384), f32),
        pltpu.VMEM((16, 8, 256), f32),
        dma((12,)),
        dma((N_ANG, 2)),
        dma((N_ANG, 2)),
        dma((2,)),
        dma((N_ANG,)),
        dma((N_ANG, 2)),
        dma((N_ANG, 2)),
        dma((N_ANG,)),
        dma((N_ANG,)),
        dma((2,)),
        dma((2,)),
        dma((N_ANG,)),
        dma((N_ANG,)),
        dma,
    ]
    return pl.pallas_call(
        functools.partial(body, sizes),
        name="laminography",
        out_shape=jax.ShapeDtypeStruct(volume.shape, f32),
        in_specs=[pl.BlockSpec(memory_space=pl.ANY)] * 9,
        out_specs=pl.BlockSpec(memory_space=pl.ANY),
        scratch_shapes=scratch,
        compiler_params=pltpu.CompilerParams(
            collective_id=0, has_side_effects=True, vmem_limit_bytes=60 << 20
        ),
    )(
        spectrum_data.reshape(2 * lines, samples),
        offsets.reshape(1, samples),
        view_index.reshape(1, samples),
        kernel,
        view_weight.reshape(1, views),
        volume,
        multiplier,
        jnp.asarray(main),
        jnp.asarray(edge),
    )


def solution(mesh):
    placed = (
        P(None, None, "gy", "ang"),
        P("ang"),
        P("ang"),
        P(None, "ang"),
        P(),
        P("ang", "gy", "gx"),
        P("ang", "gy", "gx"),
    )
    sizes = (1024 * mesh.shape["gx"], mesh.shape["gy"], mesh.shape["gx"])
    return jax.shard_map(
        functools.partial(per_device, sizes),
        mesh=mesh,
        in_specs=placed,
        out_specs=P("ang", "gy", "gx"),
        check_vma=False,
    )
```

```python
import functools
import math

import jax
import jax.numpy as jnp
import numpy as np
from jax import lax
from jax.experimental import pallas as pl
from jax.experimental.pallas import tpu as pltpu
from jax.sharding import PartitionSpec as P

MESH = pl.DeviceIdType.MESH
TV_STEPS = 4
dual_step = 1.0 / 12.0
N_ANG = 4
HALO = 4


def wave_constants(length, columns):
    block = length // N_ANG
    width = columns // N_ANG
    freq = np.arange(length, dtype=np.int64)

    def rows(cells):
        phase = np.mod(freq[:, None] * cells[None, :], length)
        angle = phase.astype(np.float32) * np.float32(2.0 * math.pi / length)
        cos = np.cos(angle).reshape(N_ANG, block, -1)
        sin = np.sin(angle).reshape(N_ANG, block, -1)
        return np.concatenate([cos, -sin], axis=1).astype(jnp.bfloat16)

    main = rows(np.arange(columns)).reshape(N_ANG, 2 * block, N_ANG, width)
    edge_cells = np.zeros(128, np.int64)
    for b in range(N_ANG):
        edge_cells[8 * b : 8 * b + 4] = width * (b + 1) + np.arange(4)
        edge_cells[8 * b + 4 : 8 * b + 8] = width * b - 4 + np.arange(4)
    return np.ascontiguousarray(main.transpose(0, 2, 1, 3)), rows(edge_cells)


def body(
    sizes,
    data_hbm,
    offsets_hbm,
    views_hbm,
    taps_hbm,
    weights_hbm,
    volume_hbm,
    multiplier_hbm,
    wave_hbm,
    edge_hbm,
    out_ref,
    data,
    offsets,
    views,
    taps,
    weights,
    volume,
    multiplier,
    wave,
    edge,
    table,
    joined,
    field,
    pieces,
    field_edge,
    extra,
    part_send,
    part_recv,
    strip_send,
    strip_recv,
    turned,
    scaled,
    flows,
    done,
    result,
    in_sem,
    ve_ssem,
    ve_rsem,
    pt_ssem,
    pt_rsem,
    st_ssem,
    st_rsem,
    hl_ssem,
    hl_rsem,
    out_ssem,
    out_rsem,
    own_sem,
):
    length, n_gy, n_gx = sizes
    block = length // N_ANG
    a, y, g = lax.axis_index("ang"), lax.axis_index("gy"), lax.axis_index("gx")
    peers = {d: lax.rem(a + d, N_ANG) for d in range(N_ANG)}

    barrier = pltpu.get_barrier_semaphore()

    def greet(where):
        pl.semaphore_signal(barrier, inc=1, device_id=where, device_id_type=MESH)

    for d in range(1, N_ANG):
        greet((peers[d], y, g))

    @pl.when(y > 0)
    def _():
        greet((a, y - 1, g))

    @pl.when(y < n_gy - 1)
    def _():
        greet((a, y + 1, g))

    @pl.when(jnp.logical_and(a == 0, g > 0))
    def _():
        for other in range(N_ANG):
            greet((other, y, g - 1))

    @pl.when(jnp.logical_and(a == N_ANG - 1, g < n_gx - 1))
    def _():
        for other in range(N_ANG):
            greet((other, y, g + 1))

    def fetch(src, dst, k):
        return pltpu.make_async_copy(src, dst, in_sem.at[k])

    small = [
        fetch(offsets_hbm, offsets, 0),
        fetch(views_hbm, views, 1),
        fetch(taps_hbm, taps, 2),
        fetch(weights_hbm, weights, 3),
        fetch(data_hbm, data, 4),
    ]
    fields = [fetch(volume_hbm, volume, 5), fetch(multiplier_hbm, multiplier, 6)]
    waves = {
        d: fetch(wave_hbm.at[a, peers[d]], wave.at[d], 7 + d) for d in range(N_ANG)
    }
    edges = fetch(edge_hbm.at[a], edge, 11)
    for copy in small + fields + [waves[2], waves[1], waves[3], edges, waves[0]]:
        copy.start()

    @pl.when(y == 0)
    def _():
        scaled[0:HALO] = jnp.zeros((HALO, 16, 384), jnp.float32)

    @pl.when(y == n_gy - 1)
    def _():
        scaled[8 + HALO :] = jnp.zeros((HALO, 16, 384), jnp.float32)

    turned[...] = jnp.zeros((128, 128), jnp.float32)
    extra[...] = jnp.zeros((8, 16, 128), jnp.float32)
    pieces[96:128] = jnp.zeros((32, 1024), jnp.bfloat16)

    for copy in small:
        copy.wait()
    for h in range(11):
        table[h : h + 1, :] = weights[pl.ds(128 * h, 128)].reshape(1, 128)
    tail = weights.shape[0] - 128
    table[11:12, :] = weights[pl.ds(tail, 128)].reshape(1, 128)
    table[12:16, :] = jnp.zeros((4, 128), jnp.float32)
    full = table[...]
    high = full.astype(jnp.bfloat16)
    rest = full - high.astype(jnp.float32)
    mid = rest.astype(jnp.bfloat16)
    low = (rest - mid.astype(jnp.float32)).astype(jnp.bfloat16)
    ids = views[...]
    group = jnp.minimum(lax.shift_right_logical(ids, 7), 11)
    within = jnp.where(group == 11, ids - tail, ids - group * 128)
    hot = (lax.broadcasted_iota(jnp.int32, (128, 512), 0) == within).astype(jnp.float32)
    hot = hot.astype(jnp.bfloat16)
    picked = (
        jnp.dot(high, hot, preferred_element_type=jnp.float32)
        + jnp.dot(mid, hot, preferred_element_type=jnp.float32)
        + jnp.dot(low, hot, preferred_element_type=jnp.float32)
    )
    of_group = lax.broadcasted_iota(jnp.int32, (16, 512), 0) == group
    weight = jnp.sum(jnp.where(of_group, picked, 0.0), axis=0, keepdims=True)
    coefs = weight * taps[...]

    line_out = lax.broadcasted_iota(jnp.int32, (128, 128), 0)
    line_in = lax.broadcasted_iota(jnp.int32, (128, 128), 1)
    order = lax.rem(line_out, 16) * 8 + lax.div(line_out, 16)
    order = (line_in == order).astype(jnp.float32).astype(jnp.bfloat16)
    for c in range(2):
        data[128 * c : 128 * c + 128] = jnp.dot(
            order, data[128 * c : 128 * c + 128], preferred_element_type=jnp.float32
        ).astype(jnp.bfloat16)

    turn = g * (4 * 1024 // length)
    firsts = offsets[...]
    for i in range(block // 256):
        base = 256 * i
        away = lax.broadcasted_iota(jnp.int32, (256, 512), 0) + base - firsts
        spread = jnp.zeros((256, 512), jnp.float32)
        for t in range(4):
            spread = jnp.where(away == t, coefs[t : t + 1], spread)
        gridded = lax.dot_general(
            data[...],
            spread.astype(jnp.bfloat16),
            (((1,), (1,)), ((), ())),
            preferred_element_type=jnp.float32,
        )
        re, im = gridded[:128], gridded[128:]
        quarter = jnp.bitwise_and(
            (lax.broadcasted_iota(jnp.int32, (1, 256), 1) + base) * turn, 3
        )
        odd = jnp.bitwise_and(quarter, 1) == 1
        re_sign = jnp.where(jnp.logical_or(quarter == 1, quarter == 2), -1.0, 1.0)
        im_sign = jnp.where(quarter >= 2, -1.0, 1.0)
        joined[:, base : base + 256] = (jnp.where(odd, im, re) * re_sign).astype(jnp.bfloat16)
        joined[:, base + block : base + block + 256] = (
            jnp.where(odd, re, im) * im_sign
        ).astype(jnp.bfloat16)

    for copy in fields:
        copy.wait()
    field[...] = volume[...] + multiplier[...]
    rest = (-(length**0.5)) * field[...].reshape(32, 1024)
    for j in range(3):
        piece = rest.astype(jnp.bfloat16)
        pieces[32 * j : 32 * j + 32] = piece
        rest = rest - piece.astype(jnp.float32)
    held_line = lax.broadcasted_iota(jnp.int32, (128, 128), 1)
    line = lax.broadcasted_iota(jnp.int32, (128, 128), 0)
    held = jnp.bitwise_and(held_line, 31)
    home = lax.rem(held, 8) * 16 + lax.div(held, 8) + 4 * a
    own_lines = jnp.where(jnp.logical_and(line == home, held_line < 96), 1.0, 0.0)
    own_lines = own_lines.astype(jnp.bfloat16)

    def transform(d):
        cells = pl.ds(pl.multiple_of(256 * peers[d], 256), 256)
        part_send[d] = jnp.dot(
            joined[...], wave[d], preferred_element_type=jnp.float32
        ) + jnp.dot(own_lines, pieces[:, cells], preferred_element_type=jnp.float32)

    waves[2].wait()
    transform(2)
    greeted = (
        N_ANG - 1
        + (y > 0).astype(jnp.int32)
        + (y < n_gy - 1).astype(jnp.int32)
        + (g > 0).astype(jnp.int32)
        + (g < n_gx - 1).astype(jnp.int32)
    )
    pl.semaphore_wait(barrier, greeted)

    def remote(src, dst, ssem, rsem, where):
        return pltpu.make_async_remote_copy(
            src_ref=src,
            dst_ref=dst,
            send_sem=ssem,
            recv_sem=rsem,
            device_id=where,
            device_id_type=MESH,
        )

    def part_copy(d, h):
        lines = pl.ds(64 * h, 64)
        return remote(
            part_send.at[d, lines],
            part_recv.at[d, lines],
            pt_ssem.at[d, h],
            pt_rsem.at[d, h],
            (peers[d], y, g),
        )

    def strip_copy(d):
        return remote(
            strip_send.at[peers[d]],
            strip_recv.at[d],
            st_ssem.at[d],
            st_rsem.at[d],
            (peers[d], y, g),
        )

    def edge_copy(up, place, target):
        tile = 1024 - 128 if up else 0
        return remote(
            field.at[:, :, pl.ds(tile, 128)],
            field_edge.at[pl.ds(4 * place, 4)],
            ve_ssem.at[0 if up else 1],
            ve_rsem.at[place],
            target,
        )

    @pl.when(g < n_gx - 1)
    def _():
        edge_copy(True, a, (0, y, g + 1)).start()

    @pl.when(g > 0)
    def _():
        edge_copy(False, a, (N_ANG - 1, y, g - 1)).start()

    part_copy(2, 0).start()
    part_copy(2, 1).start()

    for d in (1, 3):
        waves[d].wait()
        transform(d)
        part_copy(d, 0).start()
        part_copy(d, 1).start()
    edges.wait()
    slot = lax.broadcasted_iota(jnp.int32, (1, 128), 1)
    near = jnp.bitwise_and(slot, 7)
    cell = 32 * (slot - near) + jnp.where(near < 4, 256 + near, near - 8)
    chosen = lax.broadcasted_iota(jnp.int32, (1024, 128), 0) == cell
    chosen = jnp.where(jnp.logical_and(chosen, slot < 32), 1.0, 0.0).astype(jnp.bfloat16)
    near_pieces = jnp.dot(pieces[...], chosen, preferred_element_type=jnp.float32)
    strips = jnp.dot(joined[...], edge[...], preferred_element_type=jnp.float32) + jnp.dot(
        own_lines, near_pieces.astype(jnp.bfloat16), preferred_element_type=jnp.float32
    )
    strips = jnp.transpose(strips)
    for b in range(N_ANG):
        strip_send[b] = strips[8 * b : 8 * b + 8]
    for d in (2, 1, 3):
        strip_copy(d).start()
    waves[0].wait()
    transform(0)

    takes_low = jnp.logical_and(a == 0, g > 0)
    takes_high = jnp.logical_and(a == N_ANG - 1, g < n_gx - 1)

    @pl.when(jnp.logical_or(takes_low, takes_high))
    def _():
        for place in range(N_ANG):
            edge_copy(True, place, (0, y, g)).wait_recv()
        at_low = lax.broadcasted_iota(jnp.int32, (16, 8, 128), 2) < 64
        shown = jnp.logical_xor(at_low, takes_low)
        field_edge[...] = jnp.where(shown, field_edge[...], 0.0)
        for half in range(2):
            extra[:, pl.ds(8 * half, 8), :] = jnp.swapaxes(
                field_edge[pl.ds(8 * half, 8)], 0, 1
            )

    for d in range(1, N_ANG):
        strip_copy(d).wait_recv()
    strip = (strip_send[a] + strip_recv[1]) + (strip_recv[3] + strip_recv[2])
    sub = lax.broadcasted_iota(jnp.int32, (8, 128), 0)
    turned[0:8] = jnp.where(sub < 4, strip, 0.0)
    turned[120:128] = jnp.where(sub < 4, 0.0, strip)
    turned[...] = jnp.transpose(turned[...])
    unit = 2.0 * length**-0.5
    lower_dev, upper_dev = (a, y - 1, g), (a, y + 1, g)
    below = remote(
        scaled.at[pl.ds(HALO, HALO)],
        scaled.at[pl.ds(HALO + 8, HALO)],
        hl_ssem.at[0],
        hl_rsem.at[0],
        lower_dev,
    )
    above = remote(
        scaled.at[pl.ds(8, HALO)],
        scaled.at[pl.ds(0, HALO)],
        hl_ssem.at[1],
        hl_rsem.at[1],
        upper_dev,
    )
    for h in range(2):
        for d in range(1, N_ANG):
            part_copy(d, h).wait_recv()

        for i in range(4 * h, 4 * h + 4):
            lines = slice(16 * i, 16 * i + 16)
            total = (part_send[0, lines] + part_recv[1, lines]) + (
                part_recv[3, lines] + part_recv[2, lines]
            )
            beside = extra[i]
            scaled[HALO + i, :, 0:256] = total * -unit
            scaled[HALO + i, :, 256:384] = (beside + beside) - unit * turned[lines]
        if h == 0:

            @pl.when(y > 0)
            def _():
                below.start()

        else:

            @pl.when(y < n_gy - 1)
            def _():
                above.start()

    lane = lax.broadcasted_iota(jnp.int32, (16, 384), 1)
    plane = lax.broadcasted_iota(jnp.int32, (16, 384), 0)
    first = jnp.logical_and(a == 0, g == 0)
    last = jnp.logical_and(a == N_ANG - 1, g == n_gx - 1)
    closed = jnp.logical_or(
        jnp.logical_and(lane == 383, first), jnp.logical_and(lane == 255, last)
    )
    cell_step = jnp.where(closed, 0.0, dual_step)
    plane_step = jnp.where(plane == 15, 0.0, dual_step)
    lowest = plane == 0
    row_steps = {
        3: jnp.where(y == 0, 0.0, dual_step),
        11: jnp.where(y == n_gy - 1, 0.0, dual_step),
    }

    def divergence(k, r):
        q0, q1, q2 = (flows[k, c, r] for c in range(3))
        below_plane = jnp.where(lowest, 0.0, pltpu.roll(q0, 1, 0))
        return (
            (q0 - below_plane) + (q1 - flows[k, 1, r - 1]) + (q2 - pltpu.roll(q2, 1, 1))
        )

    def target(k, r):
        if k == 0:
            return -scaled[r]
        return divergence(k - 1, r) - scaled[r]

    def sweep(k, rows):
        targets = {}
        for r in rows:
            for near in (r, r + 1):
                if near not in targets:
                    targets[near] = target(k, near)
            here = targets[r]
            g0 = (pltpu.roll(here, 15, 0) - here) * plane_step
            g1 = (targets[r + 1] - here) * row_steps.get(r, dual_step)
            g2 = (pltpu.roll(here, 383, 1) - here) * cell_step
            square = (g0 * g0 + g1 * g1) + g2 * g2
            norm = square * lax.rsqrt(jnp.maximum(square, 1e-37))
            scale = 1.0 / (1.0 + norm)
            for c, slope in enumerate((g0, g1, g2)):
                if k > 0:
                    slope = flows[k - 1, c, r] + slope
                flows[k, c, r] = slope * scale

    for k in range(TV_STEPS):
        sweep(k, range(4 + k, 11 - k))

    @pl.when(y > 0)
    def _():
        above.wait_recv()

    @pl.when(y < n_gy - 1)
    def _():
        below.wait_recv()

    for k in range(TV_STEPS):
        pairs = zip(range(k, k + 4), range(11 - k, 15 - k))
        sweep(k, [r for pair in pairs for r in pair])
    for r in range(HALO, HALO + 8):
        rest = 0.5 * (scaled[r] - divergence(TV_STEPS - 1, r))
        done[r - HALO] = rest[:, 0:256]
    for half in range(2):
        for j in range(2):
            result[pl.ds(8 * half, 8), :, pl.ds(128 * j, 128)] = jnp.swapaxes(
                done[:, pl.ds(8 * half, 8), pl.ds(128 * j, 128)], 0, 1
            )

    def out_copy(d, column):
        return remote(
            result.at[pl.ds(4 * peers[d], 4)],
            out_ref.at[:, :, pl.ds(pl.multiple_of(256 * column, 256), 256)],
            out_ssem.at[d],
            out_rsem.at[d],
            (peers[d], y, g),
        )

    for d in (2, 1, 3):
        out_copy(d, a).start()
    own = pltpu.make_async_copy(
        result.at[pl.ds(4 * a, 4)],
        out_ref.at[:, :, pl.ds(pl.multiple_of(256 * a, 256), 256)],
        own_sem,
    )
    own.start()
    for d in range(1, N_ANG):
        part_copy(d, 0).wait_send()
        part_copy(d, 1).wait_send()
        strip_copy(d).wait_send()

    @pl.when(y > 0)
    def _():
        below.wait_send()

    @pl.when(y < n_gy - 1)
    def _():
        above.wait_send()

    @pl.when(g < n_gx - 1)
    def _():
        edge_copy(True, a, (0, y, g)).wait_send()

    @pl.when(g > 0)
    def _():
        edge_copy(False, a, (0, y, g)).wait_send()

    own.wait()
    for d in range(1, N_ANG):
        out_copy(d, a).wait_send()
        out_copy(d, lax.rem(a + N_ANG - d, N_ANG)).wait_recv()


def per_device(sizes, spectrum_data, offsets, view_index, kernel, view_weight, volume, multiplier):
    length = sizes[0]
    columns = volume.shape[2]
    samples = offsets.shape[0]
    lines = 16 * 8
    main, edge = wave_constants(length, columns)
    block = length // N_ANG
    f32, bf16, i32 = jnp.float32, jnp.bfloat16, jnp.int32
    dma = pltpu.SemaphoreType.DMA
    views = view_weight.shape[0]
    scratch = [
        pltpu.VMEM((2 * lines, samples), bf16),
        pltpu.VMEM((1, samples), i32),
        pltpu.VMEM((1, samples), i32),
        pltpu.VMEM((4, samples), f32),
        pltpu.VMEM((views,), f32),
        pltpu.VMEM((4, 8, columns), f32),
        pltpu.VMEM((4, 8, columns), f32),
        pltpu.VMEM((N_ANG, 2 * block, 256), bf16),
        pltpu.VMEM((2 * block, 128), bf16),
        pltpu.VMEM((16, 128), f32),
        pltpu.VMEM((lines, 2 * block), bf16),
        pltpu.VMEM((4, 8, columns), f32),
        pltpu.VMEM((128, columns), bf16),
        pltpu.VMEM((16, 8, 128), f32),
        pltpu.VMEM((8, 16, 128), f32),
        pltpu.VMEM((N_ANG, lines, 256), f32),
        pltpu.VMEM((N_ANG, lines, 256), f32),
        pltpu.VMEM((N_ANG, 8, 128), f32),
        pltpu.VMEM((N_ANG, 8, 128), f32),
        pltpu.VMEM((128, 128), f32),
        pltpu.VMEM((16, 16, 384), f32),
        pltpu.VMEM((TV_STEPS, 3, 16, 16, 384), f32),
        pltpu.VMEM((8, 16, 256), f32),
        pltpu.VMEM((16, 8, 256), f32),
        dma((12,)),
        dma((2,)),
        dma((N_ANG,)),
        dma((N_ANG, 2)),
        dma((N_ANG, 2)),
        dma((N_ANG,)),
        dma((N_ANG,)),
        dma((2,)),
        dma((2,)),
        dma((N_ANG,)),
        dma((N_ANG,)),
        dma,
    ]
    return pl.pallas_call(
        functools.partial(body, sizes),
        name="laminography",
        out_shape=pltpu.VMEM(volume.shape, f32),
        in_specs=[pl.BlockSpec(memory_space=pl.ANY)] * 9,
        out_specs=pl.BlockSpec(memory_space=pltpu.VMEM),
        scratch_shapes=scratch,
        compiler_params=pltpu.CompilerParams(
            collective_id=0, has_side_effects=True, vmem_limit_bytes=60 << 20
        ),
    )(
        spectrum_data.reshape(2 * lines, samples),
        offsets.reshape(1, samples),
        view_index.reshape(1, samples),
        kernel,
        view_weight,
        volume,
        multiplier,
        jnp.asarray(main),
        jnp.asarray(edge),
    )


def solution(mesh):
    placed = (
        P(None, None, "gy", "ang"),
        P("ang"),
        P("ang"),
        P(None, "ang"),
        P(),
        P("ang", "gy", "gx"),
        P("ang", "gy", "gx"),
    )
    sizes = (1024 * mesh.shape["gx"], mesh.shape["gy"], mesh.shape["gx"])
    return jax.shard_map(
        functools.partial(per_device, sizes),
        mesh=mesh,
        in_specs=placed,
        out_specs=P("ang", "gy", "gx"),
        check_vma=False,
    )
```

```python
import functools
import math

import jax
import jax.numpy as jnp
import numpy as np
from jax import lax
from jax.experimental import pallas as pl
from jax.experimental.pallas import tpu as pltpu
from jax.sharding import PartitionSpec as P

MESH = pl.DeviceIdType.MESH
TV_STEPS = 4
dual_step = 1.0 / 12.0
N_ANG = 4
HALO = 4


def wave_constants(length, columns):
    block = length // N_ANG
    width = columns // N_ANG
    freq = np.arange(length, dtype=np.int64)

    def rows(cells):
        phase = np.mod(freq[:, None] * cells[None, :], length)
        angle = phase.astype(np.float32) * np.float32(2.0 * math.pi / length)
        cos = np.cos(angle).reshape(N_ANG, block, -1)
        sin = np.sin(angle).reshape(N_ANG, block, -1)
        return np.concatenate([cos, -sin], axis=1).astype(jnp.bfloat16)

    main = rows(np.arange(columns)).reshape(N_ANG, 2 * block, N_ANG, width)
    edge_cells = np.zeros(128, np.int64)
    for b in range(N_ANG):
        edge_cells[8 * b : 8 * b + 4] = width * (b + 1) + np.arange(4)
        edge_cells[8 * b + 4 : 8 * b + 8] = width * b - 4 + np.arange(4)
    return np.ascontiguousarray(main.transpose(0, 2, 1, 3)), rows(edge_cells)


def body(
    sizes,
    data_hbm,
    offsets_hbm,
    views_hbm,
    taps_hbm,
    weights_hbm,
    volume_hbm,
    multiplier_hbm,
    wave_hbm,
    edge_hbm,
    out_ref,
    data,
    offsets,
    views,
    taps,
    weights,
    volume,
    multiplier,
    wave,
    edge,
    table,
    joined,
    field,
    pieces,
    field_edge,
    extra,
    part_send,
    part_recv,
    strip_send,
    strip_recv,
    turned,
    scaled,
    flows,
    done,
    result,
    in_sem,
    ve_ssem,
    ve_rsem,
    pt_ssem,
    pt_rsem,
    st_ssem,
    st_rsem,
    hl_ssem,
    hl_rsem,
    out_ssem,
    out_rsem,
    own_sem,
    ready_left,
    ready_right,
):
    length, n_gy, n_gx = sizes
    block = length // N_ANG
    a, y, g = lax.axis_index("ang"), lax.axis_index("gy"), lax.axis_index("gx")
    peers = {d: lax.rem(a + d, N_ANG) for d in range(N_ANG)}

    middle = n_gx // 2
    up_left = jnp.logical_and(g > 0, g < middle + 1)
    down_left = g > middle
    up_right = g < middle
    down_right = jnp.logical_and(g > middle - 1, g < n_gx - 1)
    answers_left = jnp.logical_and(a == 0, up_left)
    answers_right = jnp.logical_and(a == N_ANG - 1, down_right)
    barrier = pltpu.get_barrier_semaphore()

    def greet(where):
        pl.semaphore_signal(barrier, inc=1, device_id=where, device_id_type=MESH)

    for d in range(1, N_ANG):
        greet((peers[d], y, g))

    @pl.when(y > 0)
    def _():
        greet((a, y - 1, g))

    @pl.when(y < n_gy - 1)
    def _():
        greet((a, y + 1, g))

    @pl.when(up_right)
    def _():
        greet((0, y, g + 1))

    @pl.when(down_left)
    def _():
        greet((N_ANG - 1, y, g - 1))

    @pl.when(jnp.logical_and(a == 0, down_left))
    def _():
        for other in range(N_ANG):
            greet((other, y, g - 1))

    @pl.when(jnp.logical_and(a == N_ANG - 1, up_right))
    def _():
        for other in range(N_ANG):
            greet((other, y, g + 1))

    def fetch(src, dst, k):
        return pltpu.make_async_copy(src, dst, in_sem.at[k])

    small = [
        fetch(offsets_hbm, offsets, 0),
        fetch(views_hbm, views, 1),
        fetch(taps_hbm, taps, 2),
        fetch(weights_hbm, weights, 3),
        fetch(data_hbm, data, 4),
    ]
    fields = [fetch(volume_hbm, volume, 5), fetch(multiplier_hbm, multiplier, 6)]
    waves = {
        d: fetch(wave_hbm.at[a, peers[d]], wave.at[d], 7 + d) for d in range(N_ANG)
    }
    edges = fetch(edge_hbm.at[a], edge, 11)
    for copy in small + fields + [waves[2], waves[1], waves[3], edges, waves[0]]:
        copy.start()

    @pl.when(y == 0)
    def _():
        scaled[0:HALO] = jnp.zeros((HALO, 16, 384), jnp.float32)

    @pl.when(y == n_gy - 1)
    def _():
        scaled[8 + HALO :] = jnp.zeros((HALO, 16, 384), jnp.float32)

    turned[...] = jnp.zeros((128, 128), jnp.float32)
    extra[...] = jnp.zeros((8, 16, 128), jnp.float32)
    pieces[96:128] = jnp.zeros((32, 1024), jnp.bfloat16)

    for copy in small:
        copy.wait()
    for h in range(11):
        table[h : h + 1, :] = weights[pl.ds(128 * h, 128)].reshape(1, 128)
    tail = weights.shape[0] - 128
    table[11:12, :] = weights[pl.ds(tail, 128)].reshape(1, 128)
    table[12:16, :] = jnp.zeros((4, 128), jnp.float32)
    full = table[...]
    high = full.astype(jnp.bfloat16)
    rest = full - high.astype(jnp.float32)
    mid = rest.astype(jnp.bfloat16)
    low = (rest - mid.astype(jnp.float32)).astype(jnp.bfloat16)
    ids = views[...]
    group = jnp.minimum(lax.shift_right_logical(ids, 7), 11)
    within = jnp.where(group == 11, ids - tail, ids - group * 128)
    hot = (lax.broadcasted_iota(jnp.int32, (128, 512), 0) == within).astype(jnp.float32)
    hot = hot.astype(jnp.bfloat16)
    picked = (
        jnp.dot(high, hot, preferred_element_type=jnp.float32)
        + jnp.dot(mid, hot, preferred_element_type=jnp.float32)
        + jnp.dot(low, hot, preferred_element_type=jnp.float32)
    )
    of_group = lax.broadcasted_iota(jnp.int32, (16, 512), 0) == group
    weight = jnp.sum(jnp.where(of_group, picked, 0.0), axis=0, keepdims=True)
    coefs = weight * taps[...]

    line_out = lax.broadcasted_iota(jnp.int32, (128, 128), 0)
    line_in = lax.broadcasted_iota(jnp.int32, (128, 128), 1)
    order = lax.rem(line_out, 16) * 8 + lax.div(line_out, 16)
    order = (line_in == order).astype(jnp.float32).astype(jnp.bfloat16)
    for c in range(2):
        data[128 * c : 128 * c + 128] = jnp.dot(
            order, data[128 * c : 128 * c + 128], preferred_element_type=jnp.float32
        ).astype(jnp.bfloat16)

    turn = g * (4 * 1024 // length)
    firsts = offsets[...]
    for i in range(block // 256):
        base = 256 * i
        away = lax.broadcasted_iota(jnp.int32, (256, 512), 0) + base - firsts
        spread = jnp.zeros((256, 512), jnp.float32)
        for t in range(4):
            spread = jnp.where(away == t, coefs[t : t + 1], spread)
        gridded = lax.dot_general(
            data[...],
            spread.astype(jnp.bfloat16),
            (((1,), (1,)), ((), ())),
            preferred_element_type=jnp.float32,
        )
        re, im = gridded[:128], gridded[128:]
        quarter = jnp.bitwise_and(
            (lax.broadcasted_iota(jnp.int32, (1, 256), 1) + base) * turn, 3
        )
        odd = jnp.bitwise_and(quarter, 1) == 1
        re_sign = jnp.where(jnp.logical_or(quarter == 1, quarter == 2), -1.0, 1.0)
        im_sign = jnp.where(quarter >= 2, -1.0, 1.0)
        joined[:, base : base + 256] = (jnp.where(odd, im, re) * re_sign).astype(jnp.bfloat16)
        joined[:, base + block : base + block + 256] = (
            jnp.where(odd, re, im) * im_sign
        ).astype(jnp.bfloat16)

    for copy in fields:
        copy.wait()
    field[...] = volume[...] + multiplier[...]
    rest = (-(length**0.5)) * field[...].reshape(32, 1024)
    for j in range(3):
        piece = rest.astype(jnp.bfloat16)
        pieces[32 * j : 32 * j + 32] = piece
        rest = rest - piece.astype(jnp.float32)
    held_line = lax.broadcasted_iota(jnp.int32, (128, 128), 1)
    line = lax.broadcasted_iota(jnp.int32, (128, 128), 0)
    held = jnp.bitwise_and(held_line, 31)
    home = lax.rem(held, 8) * 16 + lax.div(held, 8) + 4 * a
    own_lines = jnp.where(jnp.logical_and(line == home, held_line < 96), 1.0, 0.0)
    own_lines = own_lines.astype(jnp.bfloat16)

    def transform(d):
        cells = pl.ds(pl.multiple_of(256 * peers[d], 256), 256)
        part_send[d] = jnp.dot(
            joined[...], wave[d], preferred_element_type=jnp.float32
        ) + jnp.dot(own_lines, pieces[:, cells], preferred_element_type=jnp.float32)

    waves[2].wait()
    transform(2)
    greeted = (
        N_ANG - 1
        + (y > 0).astype(jnp.int32)
        + (y < n_gy - 1).astype(jnp.int32)
        + up_left.astype(jnp.int32)
        + down_right.astype(jnp.int32)
        + N_ANG * answers_left.astype(jnp.int32)
        + N_ANG * answers_right.astype(jnp.int32)
    )
    pl.semaphore_wait(barrier, greeted)

    def answer(semaphore, where):
        pl.semaphore_signal(semaphore, inc=1, device_id=where, device_id_type=MESH)

    @pl.when(answers_left)
    def _():
        for other in range(N_ANG):
            answer(ready_right, (other, y, g - 1))

    @pl.when(answers_right)
    def _():
        for other in range(N_ANG):
            answer(ready_left, (other, y, g + 1))

    def remote(src, dst, ssem, rsem, where):
        return pltpu.make_async_remote_copy(
            src_ref=src,
            dst_ref=dst,
            send_sem=ssem,
            recv_sem=rsem,
            device_id=where,
            device_id_type=MESH,
        )

    def part_copy(d, h):
        lines = pl.ds(64 * h, 64)
        return remote(
            part_send.at[d, lines],
            part_recv.at[d, lines],
            pt_ssem.at[d, h],
            pt_rsem.at[d, h],
            (peers[d], y, g),
        )

    def strip_copy(d):
        return remote(
            strip_send.at[peers[d]],
            strip_recv.at[d],
            st_ssem.at[d],
            st_rsem.at[d],
            (peers[d], y, g),
        )

    def edge_copy(up, place, target):
        tile = 1024 - 128 if up else 0
        return remote(
            field.at[:, :, pl.ds(tile, 128)],
            field_edge.at[pl.ds(4 * place, 4)],
            ve_ssem.at[0 if up else 1],
            ve_rsem.at[place],
            target,
        )

    @pl.when(down_right)
    def _():
        edge_copy(True, a, (0, y, g + 1)).start()

    @pl.when(up_left)
    def _():
        edge_copy(False, a, (N_ANG - 1, y, g - 1)).start()

    takes_low = jnp.logical_and(a == 0, g > 0)
    takes_high = jnp.logical_and(a == N_ANG - 1, g < n_gx - 1)
    takes = jnp.logical_or(takes_low, takes_high)

    def send_answered(which):
        @pl.when(jnp.logical_and(which, up_right))
        def _():
            pl.semaphore_wait(ready_right, 1)
            edge_copy(True, a, (0, y, g + 1)).start()

    part_copy(2, 0).start()
    part_copy(2, 1).start()

    for d in (1, 3):
        waves[d].wait()
        transform(d)
        part_copy(d, 0).start()
        part_copy(d, 1).start()
    edges.wait()
    slot = lax.broadcasted_iota(jnp.int32, (1, 128), 1)
    near = jnp.bitwise_and(slot, 7)
    cell = 32 * (slot - near) + jnp.where(near < 4, 256 + near, near - 8)
    chosen = lax.broadcasted_iota(jnp.int32, (1024, 128), 0) == cell
    chosen = jnp.where(jnp.logical_and(chosen, slot < 32), 1.0, 0.0).astype(jnp.bfloat16)
    near_pieces = jnp.dot(pieces[...], chosen, preferred_element_type=jnp.float32)
    strips = jnp.dot(joined[...], edge[...], preferred_element_type=jnp.float32) + jnp.dot(
        own_lines, near_pieces.astype(jnp.bfloat16), preferred_element_type=jnp.float32
    )
    strips = jnp.transpose(strips)
    for b in range(N_ANG):
        strip_send[b] = strips[8 * b : 8 * b + 8]
    for d in (2, 1, 3):
        strip_copy(d).start()
    waves[0].wait()
    transform(0)

    @pl.when(down_left)
    def _():
        pl.semaphore_wait(ready_left, 1)
        edge_copy(False, a, (N_ANG - 1, y, g - 1)).start()

    send_answered(takes)

    @pl.when(takes)
    def _():
        for place in range(N_ANG):
            edge_copy(True, place, (0, y, g)).wait_recv()
        at_low = lax.broadcasted_iota(jnp.int32, (16, 8, 128), 2) < 64
        shown = jnp.logical_xor(at_low, takes_low)
        field_edge[...] = jnp.where(shown, field_edge[...], 0.0)
        for half in range(2):
            extra[:, pl.ds(8 * half, 8), :] = jnp.swapaxes(
                field_edge[pl.ds(8 * half, 8)], 0, 1
            )

    for d in range(1, N_ANG):
        strip_copy(d).wait_recv()
    strip = (strip_send[a] + strip_recv[1]) + (strip_recv[3] + strip_recv[2])
    sub = lax.broadcasted_iota(jnp.int32, (8, 128), 0)
    turned[0:8] = jnp.where(sub < 4, strip, 0.0)
    turned[120:128] = jnp.where(sub < 4, 0.0, strip)
    turned[...] = jnp.transpose(turned[...])
    unit = 2.0 * length**-0.5
    lower_dev, upper_dev = (a, y - 1, g), (a, y + 1, g)
    below = remote(
        scaled.at[pl.ds(HALO, HALO)],
        scaled.at[pl.ds(HALO + 8, HALO)],
        hl_ssem.at[0],
        hl_rsem.at[0],
        lower_dev,
    )
    above = remote(
        scaled.at[pl.ds(8, HALO)],
        scaled.at[pl.ds(0, HALO)],
        hl_ssem.at[1],
        hl_rsem.at[1],
        upper_dev,
    )
    for h in range(2):
        for d in range(1, N_ANG):
            part_copy(d, h).wait_recv()

        for i in range(4 * h, 4 * h + 4):
            lines = slice(16 * i, 16 * i + 16)
            total = (part_send[0, lines] + part_recv[1, lines]) + (
                part_recv[3, lines] + part_recv[2, lines]
            )
            beside = extra[i]
            scaled[HALO + i, :, 0:256] = total * -unit
            scaled[HALO + i, :, 256:384] = (beside + beside) - unit * turned[lines]
        if h == 0:

            @pl.when(y > 0)
            def _():
                below.start()

        else:

            @pl.when(y < n_gy - 1)
            def _():
                above.start()

    send_answered(jnp.logical_not(takes))

    lane = lax.broadcasted_iota(jnp.int32, (16, 384), 1)
    plane = lax.broadcasted_iota(jnp.int32, (16, 384), 0)
    first = jnp.logical_and(a == 0, g == 0)
    last = jnp.logical_and(a == N_ANG - 1, g == n_gx - 1)
    closed = jnp.logical_or(
        jnp.logical_and(lane == 383, first), jnp.logical_and(lane == 255, last)
    )
    cell_step = jnp.where(closed, 0.0, dual_step)
    plane_step = jnp.where(plane == 15, 0.0, dual_step)
    lowest = plane == 0
    row_steps = {
        3: jnp.where(y == 0, 0.0, dual_step),
        11: jnp.where(y == n_gy - 1, 0.0, dual_step),
    }

    def divergence(k, r):
        q0, q1, q2 = (flows[k, c, r] for c in range(3))
        below_plane = jnp.where(lowest, 0.0, pltpu.roll(q0, 1, 0))
        return (
            (q0 - below_plane) + (q1 - flows[k, 1, r - 1]) + (q2 - pltpu.roll(q2, 1, 1))
        )

    def target(k, r):
        if k == 0:
            return -scaled[r]
        return divergence(k - 1, r) - scaled[r]

    def sweep(k, rows):
        targets = {}
        for r in rows:
            for near in (r, r + 1):
                if near not in targets:
                    targets[near] = target(k, near)
            here = targets[r]
            g0 = (pltpu.roll(here, 15, 0) - here) * plane_step
            g1 = (targets[r + 1] - here) * row_steps.get(r, dual_step)
            g2 = (pltpu.roll(here, 383, 1) - here) * cell_step
            square = (g0 * g0 + g1 * g1) + g2 * g2
            norm = square * lax.rsqrt(jnp.maximum(square, 1e-37))
            scale = 1.0 / (1.0 + norm)
            for c, slope in enumerate((g0, g1, g2)):
                if k > 0:
                    slope = flows[k - 1, c, r] + slope
                flows[k, c, r] = slope * scale

    for k in range(TV_STEPS):
        sweep(k, range(4 + k, 11 - k))

    @pl.when(y > 0)
    def _():
        above.wait_recv()

    @pl.when(y < n_gy - 1)
    def _():
        below.wait_recv()

    for k in range(TV_STEPS):
        pairs = zip(range(k, k + 4), range(11 - k, 15 - k))
        sweep(k, [r for pair in pairs for r in pair])
    for r in range(HALO, HALO + 8):
        rest = 0.5 * (scaled[r] - divergence(TV_STEPS - 1, r))
        done[r - HALO] = rest[:, 0:256]
    for half in range(2):
        for j in range(2):
            result[pl.ds(8 * half, 8), :, pl.ds(128 * j, 128)] = jnp.swapaxes(
                done[:, pl.ds(8 * half, 8), pl.ds(128 * j, 128)], 0, 1
            )

    def out_copy(d, column):
        return remote(
            result.at[pl.ds(4 * peers[d], 4)],
            out_ref.at[:, :, pl.ds(pl.multiple_of(256 * column, 256), 256)],
            out_ssem.at[d],
            out_rsem.at[d],
            (peers[d], y, g),
        )

    for d in (2, 1, 3):
        out_copy(d, a).start()
    own = pltpu.make_async_copy(
        result.at[pl.ds(4 * a, 4)],
        out_ref.at[:, :, pl.ds(pl.multiple_of(256 * a, 256), 256)],
        own_sem,
    )
    own.start()
    for d in range(1, N_ANG):
        part_copy(d, 0).wait_send()
        part_copy(d, 1).wait_send()
        strip_copy(d).wait_send()

    @pl.when(y > 0)
    def _():
        below.wait_send()

    @pl.when(y < n_gy - 1)
    def _():
        above.wait_send()

    @pl.when(g < n_gx - 1)
    def _():
        edge_copy(True, a, (0, y, g)).wait_send()

    @pl.when(g > 0)
    def _():
        edge_copy(False, a, (0, y, g)).wait_send()

    own.wait()
    for d in range(1, N_ANG):
        out_copy(d, a).wait_send()
        out_copy(d, lax.rem(a + N_ANG - d, N_ANG)).wait_recv()


def per_device(sizes, spectrum_data, offsets, view_index, kernel, view_weight, volume, multiplier):
    length = sizes[0]
    columns = volume.shape[2]
    samples = offsets.shape[0]
    lines = 16 * 8
    main, edge = wave_constants(length, columns)
    block = length // N_ANG
    f32, bf16, i32 = jnp.float32, jnp.bfloat16, jnp.int32
    dma = pltpu.SemaphoreType.DMA
    views = view_weight.shape[0]
    scratch = [
        pltpu.VMEM((2 * lines, samples), bf16),
        pltpu.VMEM((1, samples), i32),
        pltpu.VMEM((1, samples), i32),
        pltpu.VMEM((4, samples), f32),
        pltpu.VMEM((views,), f32),
        pltpu.VMEM((4, 8, columns), f32),
        pltpu.VMEM((4, 8, columns), f32),
        pltpu.VMEM((N_ANG, 2 * block, 256), bf16),
        pltpu.VMEM((2 * block, 128), bf16),
        pltpu.VMEM((16, 128), f32),
        pltpu.VMEM((lines, 2 * block), bf16),
        pltpu.VMEM((4, 8, columns), f32),
        pltpu.VMEM((128, columns), bf16),
        pltpu.VMEM((16, 8, 128), f32),
        pltpu.VMEM((8, 16, 128), f32),
        pltpu.VMEM((N_ANG, lines, 256), f32),
        pltpu.VMEM((N_ANG, lines, 256), f32),
        pltpu.VMEM((N_ANG, 8, 128), f32),
        pltpu.VMEM((N_ANG, 8, 128), f32),
        pltpu.VMEM((128, 128), f32),
        pltpu.VMEM((16, 16, 384), f32),
        pltpu.VMEM((TV_STEPS, 3, 16, 16, 384), f32),
        pltpu.VMEM((8, 16, 256), f32),
        pltpu.VMEM((16, 8, 256), f32),
        dma((12,)),
        dma((2,)),
        dma((N_ANG,)),
        dma((N_ANG, 2)),
        dma((N_ANG, 2)),
        dma((N_ANG,)),
        dma((N_ANG,)),
        dma((2,)),
        dma((2,)),
        dma((N_ANG,)),
        dma((N_ANG,)),
        dma,
        pltpu.SemaphoreType.REGULAR,
        pltpu.SemaphoreType.REGULAR,
    ]
    return pl.pallas_call(
        functools.partial(body, sizes),
        name="laminography",
        out_shape=pltpu.VMEM(volume.shape, f32),
        in_specs=[pl.BlockSpec(memory_space=pl.ANY)] * 9,
        out_specs=pl.BlockSpec(memory_space=pltpu.VMEM),
        scratch_shapes=scratch,
        compiler_params=pltpu.CompilerParams(
            collective_id=0, has_side_effects=True, vmem_limit_bytes=60 << 20
        ),
    )(
        spectrum_data.reshape(2 * lines, samples),
        offsets.reshape(1, samples),
        view_index.reshape(1, samples),
        kernel,
        view_weight,
        volume,
        multiplier,
        jnp.asarray(main),
        jnp.asarray(edge),
    )


def solution(mesh):
    placed = (
        P(None, None, "gy", "ang"),
        P("ang"),
        P("ang"),
        P(None, "ang"),
        P(),
        P("ang", "gy", "gx"),
        P("ang", "gy", "gx"),
    )
    sizes = (1024 * mesh.shape["gx"], mesh.shape["gy"], mesh.shape["gx"])
    return jax.shard_map(
        functools.partial(per_device, sizes),
        mesh=mesh,
        in_specs=placed,
        out_specs=P("ang", "gy", "gx"),
        check_vma=False,
    )
```

```python
import functools
import math

import jax
import jax.numpy as jnp
import numpy as np
from jax import lax
from jax.experimental import pallas as pl
from jax.experimental.pallas import tpu as pltpu
from jax.sharding import PartitionSpec as P

MESH = pl.DeviceIdType.MESH
TV_STEPS = 4
dual_step = 1.0 / 12.0
N_ANG = 4
HALO = 4


def wave_constants(length, columns):
    block = length // N_ANG
    width = columns // N_ANG
    freq = np.arange(length, dtype=np.int64)

    def rows(cells):
        phase = np.mod(freq[:, None] * cells[None, :], length)
        angle = phase.astype(np.float32) * np.float32(2.0 * math.pi / length)
        cos = np.cos(angle).reshape(N_ANG, block, -1)
        sin = np.sin(angle).reshape(N_ANG, block, -1)
        return np.concatenate([cos, -sin], axis=1).astype(jnp.bfloat16)

    main = rows(np.arange(columns)).reshape(N_ANG, 2 * block, N_ANG, width)
    edge_cells = np.zeros(128, np.int64)
    for b in range(N_ANG):
        edge_cells[8 * b : 8 * b + 4] = width * (b + 1) + np.arange(4)
        edge_cells[8 * b + 4 : 8 * b + 8] = width * b - 4 + np.arange(4)
    return np.ascontiguousarray(main.transpose(0, 2, 1, 3)), rows(edge_cells)


def body(
    sizes,
    data_hbm,
    offsets_hbm,
    views_hbm,
    taps_hbm,
    weights_hbm,
    volume_hbm,
    multiplier_hbm,
    wave_hbm,
    edge_hbm,
    out_ref,
    data,
    offsets,
    views,
    taps,
    weights,
    volume,
    multiplier,
    wave,
    edge,
    table,
    joined,
    field,
    pieces,
    field_edge,
    extra,
    part_send,
    part_recv,
    strip_send,
    strip_recv,
    turned,
    scaled,
    flows,
    done,
    result,
    in_sem,
    ve_ssem,
    ve_rsem,
    pt_ssem,
    pt_rsem,
    st_ssem,
    st_rsem,
    hl_ssem,
    hl_rsem,
    out_ssem,
    out_rsem,
    own_sem,
    ready_left,
    ready_right,
):
    length, n_gy, n_gx = sizes
    block = length // N_ANG
    a, y, g = lax.axis_index("ang"), lax.axis_index("gy"), lax.axis_index("gx")
    peers = {d: lax.rem(a + d, N_ANG) for d in range(N_ANG)}

    middle = n_gx // 2
    up_left = jnp.logical_and(g > 0, g < middle + 1)
    down_left = g > middle
    up_right = g < middle
    down_right = jnp.logical_and(g > middle - 1, g < n_gx - 1)
    answers_left = jnp.logical_and(a == 0, up_left)
    answers_right = jnp.logical_and(a == N_ANG - 1, down_right)
    barrier = pltpu.get_barrier_semaphore()

    def greet(where):
        pl.semaphore_signal(barrier, inc=1, device_id=where, device_id_type=MESH)

    for d in range(1, N_ANG):
        greet((peers[d], y, g))

    @pl.when(y > 0)
    def _():
        greet((a, y - 1, g))

    @pl.when(y < n_gy - 1)
    def _():
        greet((a, y + 1, g))

    @pl.when(up_right)
    def _():
        greet((0, y, g + 1))

    @pl.when(down_left)
    def _():
        greet((N_ANG - 1, y, g - 1))

    @pl.when(jnp.logical_and(a == 0, down_left))
    def _():
        for other in range(N_ANG):
            greet((other, y, g - 1))

    @pl.when(jnp.logical_and(a == N_ANG - 1, up_right))
    def _():
        for other in range(N_ANG):
            greet((other, y, g + 1))

    def fetch(src, dst, k):
        return pltpu.make_async_copy(src, dst, in_sem.at[k])

    small = [
        fetch(offsets_hbm, offsets, 0),
        fetch(views_hbm, views, 1),
        fetch(taps_hbm, taps, 2),
        fetch(weights_hbm, weights, 3),
        fetch(data_hbm, data, 4),
    ]
    fields = [fetch(volume_hbm, volume, 5), fetch(multiplier_hbm, multiplier, 6)]
    waves = {
        d: fetch(wave_hbm.at[a, peers[d]], wave.at[d], 7 + d) for d in range(N_ANG)
    }
    edges = fetch(edge_hbm.at[a], edge, 11)
    for copy in small + fields + [waves[2], waves[1], waves[3], edges, waves[0]]:
        copy.start()

    @pl.when(y == 0)
    def _():
        scaled[0:HALO] = jnp.zeros((HALO, 16, 384), jnp.float32)

    @pl.when(y == n_gy - 1)
    def _():
        scaled[8 + HALO :] = jnp.zeros((HALO, 16, 384), jnp.float32)

    turned[...] = jnp.zeros((128, 128), jnp.float32)
    extra[...] = jnp.zeros((8, 16, 128), jnp.float32)
    pieces[96:128] = jnp.zeros((32, 1024), jnp.bfloat16)

    for copy in small:
        copy.wait()
    for h in range(11):
        table[h : h + 1, :] = weights[pl.ds(128 * h, 128)].reshape(1, 128)
    tail = weights.shape[0] - 128
    table[11:12, :] = weights[pl.ds(tail, 128)].reshape(1, 128)
    table[12:16, :] = jnp.zeros((4, 128), jnp.float32)
    full = table[...]
    high = full.astype(jnp.bfloat16)
    rest = full - high.astype(jnp.float32)
    mid = rest.astype(jnp.bfloat16)
    low = (rest - mid.astype(jnp.float32)).astype(jnp.bfloat16)
    ids = views[...]
    group = jnp.minimum(lax.shift_right_logical(ids, 7), 11)
    within = jnp.where(group == 11, ids - tail, ids - group * 128)
    hot = (lax.broadcasted_iota(jnp.int32, (128, 512), 0) == within).astype(jnp.float32)
    hot = hot.astype(jnp.bfloat16)
    picked = (
        jnp.dot(high, hot, preferred_element_type=jnp.float32)
        + jnp.dot(mid, hot, preferred_element_type=jnp.float32)
        + jnp.dot(low, hot, preferred_element_type=jnp.float32)
    )
    of_group = lax.broadcasted_iota(jnp.int32, (16, 512), 0) == group
    weight = jnp.sum(jnp.where(of_group, picked, 0.0), axis=0, keepdims=True)
    coefs = weight * taps[...]

    line_out = lax.broadcasted_iota(jnp.int32, (128, 128), 0)
    line_in = lax.broadcasted_iota(jnp.int32, (128, 128), 1)
    order = lax.rem(line_out, 16) * 8 + lax.div(line_out, 16)
    order = (line_in == order).astype(jnp.float32).astype(jnp.bfloat16)
    for c in range(2):
        data[128 * c : 128 * c + 128] = jnp.dot(
            order, data[128 * c : 128 * c + 128], preferred_element_type=jnp.float32
        ).astype(jnp.bfloat16)

    turn = g * (4 * 1024 // length)
    firsts = offsets[...]
    for i in range(block // 256):
        base = 256 * i
        away = lax.broadcasted_iota(jnp.int32, (256, 512), 0) + base - firsts
        spread = jnp.zeros((256, 512), jnp.float32)
        for t in range(4):
            spread = jnp.where(away == t, coefs[t : t + 1], spread)
        gridded = lax.dot_general(
            data[...],
            spread.astype(jnp.bfloat16),
            (((1,), (1,)), ((), ())),
            preferred_element_type=jnp.float32,
        )
        re, im = gridded[:128], gridded[128:]
        quarter = jnp.bitwise_and(
            (lax.broadcasted_iota(jnp.int32, (1, 256), 1) + base) * turn, 3
        )
        odd = jnp.bitwise_and(quarter, 1) == 1
        re_sign = jnp.where(jnp.logical_or(quarter == 1, quarter == 2), -1.0, 1.0)
        im_sign = jnp.where(quarter >= 2, -1.0, 1.0)
        joined[:, base : base + 256] = (jnp.where(odd, im, re) * re_sign).astype(jnp.bfloat16)
        joined[:, base + block : base + block + 256] = (
            jnp.where(odd, re, im) * im_sign
        ).astype(jnp.bfloat16)

    for copy in fields:
        copy.wait()
    field[...] = volume[...] + multiplier[...]
    rest = (-(length**0.5)) * field[...].reshape(32, 1024)
    for j in range(3):
        piece = rest.astype(jnp.bfloat16)
        pieces[32 * j : 32 * j + 32] = piece
        rest = rest - piece.astype(jnp.float32)
    held_line = lax.broadcasted_iota(jnp.int32, (128, 128), 1)
    line = lax.broadcasted_iota(jnp.int32, (128, 128), 0)
    held = jnp.bitwise_and(held_line, 31)
    home = lax.rem(held, 8) * 16 + lax.div(held, 8) + 4 * a
    own_lines = jnp.where(jnp.logical_and(line == home, held_line < 96), 1.0, 0.0)
    own_lines = own_lines.astype(jnp.bfloat16)

    def transform(d):
        cells = pl.ds(pl.multiple_of(256 * peers[d], 256), 256)
        part_send[d] = jnp.dot(
            joined[...], wave[d], preferred_element_type=jnp.float32
        ) + jnp.dot(own_lines, pieces[:, cells], preferred_element_type=jnp.float32)

    waves[2].wait()
    transform(2)
    greeted = (
        N_ANG - 1
        + (y > 0).astype(jnp.int32)
        + (y < n_gy - 1).astype(jnp.int32)
        + up_left.astype(jnp.int32)
        + down_right.astype(jnp.int32)
        + N_ANG * answers_left.astype(jnp.int32)
        + N_ANG * answers_right.astype(jnp.int32)
    )
    pl.semaphore_wait(barrier, greeted)

    def answer(semaphore, where):
        pl.semaphore_signal(semaphore, inc=1, device_id=where, device_id_type=MESH)

    @pl.when(answers_left)
    def _():
        for other in range(N_ANG):
            answer(ready_right, (other, y, g - 1))

    @pl.when(answers_right)
    def _():
        for other in range(N_ANG):
            answer(ready_left, (other, y, g + 1))

    def remote(src, dst, ssem, rsem, where):
        return pltpu.make_async_remote_copy(
            src_ref=src,
            dst_ref=dst,
            send_sem=ssem,
            recv_sem=rsem,
            device_id=where,
            device_id_type=MESH,
        )

    def part_copy(d, h):
        lines = pl.ds(64 * h, 64)
        return remote(
            part_send.at[d, lines],
            part_recv.at[d, lines],
            pt_ssem.at[d, h],
            pt_rsem.at[d, h],
            (peers[d], y, g),
        )

    def strip_copy(d):
        return remote(
            strip_send.at[peers[d]],
            strip_recv.at[d],
            st_ssem.at[d],
            st_rsem.at[d],
            (peers[d], y, g),
        )

    def edge_copy(up, place, target):
        tile = 1024 - 128 if up else 0
        return remote(
            field.at[:, :, pl.ds(tile, 128)],
            field_edge.at[pl.ds(4 * place, 4)],
            ve_ssem.at[0 if up else 1],
            ve_rsem.at[place],
            target,
        )

    @pl.when(down_right)
    def _():
        edge_copy(True, a, (0, y, g + 1)).start()

    @pl.when(up_left)
    def _():
        edge_copy(False, a, (N_ANG - 1, y, g - 1)).start()

    takes_low = jnp.logical_and(a == 0, g > 0)
    takes_high = jnp.logical_and(a == N_ANG - 1, g < n_gx - 1)
    takes = jnp.logical_or(takes_low, takes_high)

    part_copy(2, 0).start()
    part_copy(2, 1).start()

    for d in (1, 3):
        waves[d].wait()
        transform(d)
        part_copy(d, 0).start()
        part_copy(d, 1).start()
    edges.wait()
    slot = lax.broadcasted_iota(jnp.int32, (1, 128), 1)
    near = jnp.bitwise_and(slot, 7)
    cell = 32 * (slot - near) + jnp.where(near < 4, 256 + near, near - 8)
    chosen = lax.broadcasted_iota(jnp.int32, (1024, 128), 0) == cell
    chosen = jnp.where(jnp.logical_and(chosen, slot < 32), 1.0, 0.0).astype(jnp.bfloat16)
    near_pieces = jnp.dot(pieces[...], chosen, preferred_element_type=jnp.float32)
    strips = jnp.dot(joined[...], edge[...], preferred_element_type=jnp.float32) + jnp.dot(
        own_lines, near_pieces.astype(jnp.bfloat16), preferred_element_type=jnp.float32
    )
    strips = jnp.transpose(strips)
    for b in range(N_ANG):
        strip_send[b] = strips[8 * b : 8 * b + 8]
    for d in (2, 1, 3):
        strip_copy(d).start()
    waves[0].wait()
    transform(0)

    @pl.when(down_left)
    def _():
        pl.semaphore_wait(ready_left, 1)
        edge_copy(False, a, (N_ANG - 1, y, g - 1)).start()

    def send_answered(which):
        @pl.when(which)
        def _():
            pl.semaphore_wait(ready_right, 1)
            edge_copy(True, a, (0, y, g + 1)).start()

    send_answered(g == middle - 1)

    for d in range(1, N_ANG):
        strip_copy(d).wait_recv()
    strip = (strip_send[a] + strip_recv[1]) + (strip_recv[3] + strip_recv[2])
    sub = lax.broadcasted_iota(jnp.int32, (8, 128), 0)
    turned[0:8] = jnp.where(sub < 4, strip, 0.0)
    turned[120:128] = jnp.where(sub < 4, 0.0, strip)
    turned[...] = jnp.transpose(turned[...])
    unit = 2.0 * length**-0.5
    lower_dev, upper_dev = (a, y - 1, g), (a, y + 1, g)
    below = remote(
        scaled.at[pl.ds(HALO, HALO)],
        scaled.at[pl.ds(HALO + 8, HALO)],
        hl_ssem.at[0],
        hl_rsem.at[0],
        lower_dev,
    )
    above = remote(
        scaled.at[pl.ds(8, HALO)],
        scaled.at[pl.ds(0, HALO)],
        hl_ssem.at[1],
        hl_rsem.at[1],
        upper_dev,
    )
    for h in range(2):
        for d in range(1, N_ANG):
            part_copy(d, h).wait_recv()

        for i in range(4 * h, 4 * h + 4):
            lines = slice(16 * i, 16 * i + 16)
            total = (part_send[0, lines] + part_recv[1, lines]) + (
                part_recv[3, lines] + part_recv[2, lines]
            )
            scaled[HALO + i, :, 0:256] = total * -unit
            scaled[HALO + i, :, 256:384] = turned[lines] * -unit
        if h == 0:

            @pl.when(jnp.logical_and(y > 0, jnp.logical_not(takes)))
            def _():
                below.start()

        else:

            @pl.when(jnp.logical_and(y < n_gy - 1, jnp.logical_not(takes)))
            def _():
                above.start()

    send_answered(g < middle - 1)

    @pl.when(takes)
    def _():
        for place in range(N_ANG):
            edge_copy(True, place, (0, y, g)).wait_recv()
        at_low = lax.broadcasted_iota(jnp.int32, (16, 8, 128), 2) < 64
        shown = jnp.logical_xor(at_low, takes_low)
        field_edge[...] = jnp.where(shown, field_edge[...], 0.0)
        for half in range(2):
            extra[:, pl.ds(8 * half, 8), :] = jnp.swapaxes(
                field_edge[pl.ds(8 * half, 8)], 0, 1
            )

    @pl.when(takes)
    def _():
        for i in range(8):
            beside = extra[i]
            own_edge = scaled[HALO + i, :, 256:384]
            scaled[HALO + i, :, 256:384] = own_edge + (beside + beside)

    @pl.when(jnp.logical_and(y > 0, takes))
    def _():
        below.start()

    @pl.when(jnp.logical_and(y < n_gy - 1, takes))
    def _():
        above.start()

    lane = lax.broadcasted_iota(jnp.int32, (16, 384), 1)
    plane = lax.broadcasted_iota(jnp.int32, (16, 384), 0)
    first = jnp.logical_and(a == 0, g == 0)
    last = jnp.logical_and(a == N_ANG - 1, g == n_gx - 1)
    closed = jnp.logical_or(
        jnp.logical_and(lane == 383, first), jnp.logical_and(lane == 255, last)
    )
    cell_step = jnp.where(closed, 0.0, dual_step)
    plane_step = jnp.where(plane == 15, 0.0, dual_step)
    lowest = plane == 0
    row_steps = {
        3: jnp.where(y == 0, 0.0, dual_step),
        11: jnp.where(y == n_gy - 1, 0.0, dual_step),
    }

    def divergence(k, r):
        q0, q1, q2 = (flows[k, c, r] for c in range(3))
        below_plane = jnp.where(lowest, 0.0, pltpu.roll(q0, 1, 0))
        return (
            (q0 - below_plane) + (q1 - flows[k, 1, r - 1]) + (q2 - pltpu.roll(q2, 1, 1))
        )

    def target(k, r):
        if k == 0:
            return -scaled[r]
        return divergence(k - 1, r) - scaled[r]

    def sweep(k, rows):
        targets = {}
        for r in rows:
            for near in (r, r + 1):
                if near not in targets:
                    targets[near] = target(k, near)
            here = targets[r]
            g0 = (pltpu.roll(here, 15, 0) - here) * plane_step
            g1 = (targets[r + 1] - here) * row_steps.get(r, dual_step)
            g2 = (pltpu.roll(here, 383, 1) - here) * cell_step
            square = (g0 * g0 + g1 * g1) + g2 * g2
            norm = square * lax.rsqrt(jnp.maximum(square, 1e-37))
            scale = 1.0 / (1.0 + norm)
            for c, slope in enumerate((g0, g1, g2)):
                if k > 0:
                    slope = flows[k - 1, c, r] + slope
                flows[k, c, r] = slope * scale

    for k in range(TV_STEPS):
        sweep(k, range(4 + k, 11 - k))

    @pl.when(y > 0)
    def _():
        above.wait_recv()

    @pl.when(y < n_gy - 1)
    def _():
        below.wait_recv()

    for k in range(TV_STEPS):
        pairs = zip(range(k, k + 4), range(11 - k, 15 - k))
        sweep(k, [r for pair in pairs for r in pair])
    for r in range(HALO, HALO + 8):
        rest = 0.5 * (scaled[r] - divergence(TV_STEPS - 1, r))
        done[r - HALO] = rest[:, 0:256]
    for half in range(2):
        for j in range(2):
            result[pl.ds(8 * half, 8), :, pl.ds(128 * j, 128)] = jnp.swapaxes(
                done[:, pl.ds(8 * half, 8), pl.ds(128 * j, 128)], 0, 1
            )

    def out_copy(d, column):
        return remote(
            result.at[pl.ds(4 * peers[d], 4)],
            out_ref.at[:, :, pl.ds(pl.multiple_of(256 * column, 256), 256)],
            out_ssem.at[d],
            out_rsem.at[d],
            (peers[d], y, g),
        )

    for d in (2, 1, 3):
        out_copy(d, a).start()
    own = pltpu.make_async_copy(
        result.at[pl.ds(4 * a, 4)],
        out_ref.at[:, :, pl.ds(pl.multiple_of(256 * a, 256), 256)],
        own_sem,
    )
    own.start()
    for d in range(1, N_ANG):
        part_copy(d, 0).wait_send()
        part_copy(d, 1).wait_send()
        strip_copy(d).wait_send()

    @pl.when(y > 0)
    def _():
        below.wait_send()

    @pl.when(y < n_gy - 1)
    def _():
        above.wait_send()

    @pl.when(g < n_gx - 1)
    def _():
        edge_copy(True, a, (0, y, g)).wait_send()

    @pl.when(g > 0)
    def _():
        edge_copy(False, a, (0, y, g)).wait_send()

    own.wait()
    for d in range(1, N_ANG):
        out_copy(d, a).wait_send()
        out_copy(d, lax.rem(a + N_ANG - d, N_ANG)).wait_recv()


def per_device(sizes, spectrum_data, offsets, view_index, kernel, view_weight, volume, multiplier):
    length = sizes[0]
    columns = volume.shape[2]
    samples = offsets.shape[0]
    lines = 16 * 8
    main, edge = wave_constants(length, columns)
    block = length // N_ANG
    f32, bf16, i32 = jnp.float32, jnp.bfloat16, jnp.int32
    dma = pltpu.SemaphoreType.DMA
    views = view_weight.shape[0]
    scratch = [
        pltpu.VMEM((2 * lines, samples), bf16),
        pltpu.VMEM((1, samples), i32),
        pltpu.VMEM((1, samples), i32),
        pltpu.VMEM((4, samples), f32),
        pltpu.VMEM((views,), f32),
        pltpu.VMEM((4, 8, columns), f32),
        pltpu.VMEM((4, 8, columns), f32),
        pltpu.VMEM((N_ANG, 2 * block, 256), bf16),
        pltpu.VMEM((2 * block, 128), bf16),
        pltpu.VMEM((16, 128), f32),
        pltpu.VMEM((lines, 2 * block), bf16),
        pltpu.VMEM((4, 8, columns), f32),
        pltpu.VMEM((128, columns), bf16),
        pltpu.VMEM((16, 8, 128), f32),
        pltpu.VMEM((8, 16, 128), f32),
        pltpu.VMEM((N_ANG, lines, 256), f32),
        pltpu.VMEM((N_ANG, lines, 256), f32),
        pltpu.VMEM((N_ANG, 8, 128), f32),
        pltpu.VMEM((N_ANG, 8, 128), f32),
        pltpu.VMEM((128, 128), f32),
        pltpu.VMEM((16, 16, 384), f32),
        pltpu.VMEM((TV_STEPS, 3, 16, 16, 384), f32),
        pltpu.VMEM((8, 16, 256), f32),
        pltpu.VMEM((16, 8, 256), f32),
        dma((12,)),
        dma((2,)),
        dma((N_ANG,)),
        dma((N_ANG, 2)),
        dma((N_ANG, 2)),
        dma((N_ANG,)),
        dma((N_ANG,)),
        dma((2,)),
        dma((2,)),
        dma((N_ANG,)),
        dma((N_ANG,)),
        dma,
        pltpu.SemaphoreType.REGULAR,
        pltpu.SemaphoreType.REGULAR,
    ]
    return pl.pallas_call(
        functools.partial(body, sizes),
        name="laminography",
        out_shape=pltpu.VMEM(volume.shape, f32),
        in_specs=[pl.BlockSpec(memory_space=pl.ANY)] * 9,
        out_specs=pl.BlockSpec(memory_space=pltpu.VMEM),
        scratch_shapes=scratch,
        compiler_params=pltpu.CompilerParams(
            collective_id=0, has_side_effects=True, vmem_limit_bytes=60 << 20
        ),
    )(
        spectrum_data.reshape(2 * lines, samples),
        offsets.reshape(1, samples),
        view_index.reshape(1, samples),
        kernel,
        view_weight,
        volume,
        multiplier,
        jnp.asarray(main),
        jnp.asarray(edge),
    )


def solution(mesh):
    placed = (
        P(None, None, "gy", "ang"),
        P("ang"),
        P("ang"),
        P(None, "ang"),
        P(),
        P("ang", "gy", "gx"),
        P("ang", "gy", "gx"),
    )
    sizes = (1024 * mesh.shape["gx"], mesh.shape["gy"], mesh.shape["gx"])
    return jax.shard_map(
        functools.partial(per_device, sizes),
        mesh=mesh,
        in_specs=placed,
        out_specs=P("ang", "gy", "gx"),
        check_vma=False,
    )
```
